32 devices in a mesh: dp: 8 (over z, x), tensor: 4 (over y, core).
Axes of the slice: x: 2, y: 2, z: 4, core: 2. Of those that a mesh axis runs over, the one named last changes fastest.
Arguments:
- hidden_in: bfloat16 [24576, 1024], P(('dp', 'tensor')), may hold values from -6 to 6
- segments: int32 [24576], P('dp'), may hold values from 0 to 80, never falling along the last dimension, each value on 1 to 800 neighbouring positions
- cotangent: bfloat16 [24576, 1024], P(('dp', 'tensor')), may hold values from -6 to 6
- w_z: bfloat16 [1024, 2048], P('dp', 'tensor'), may hold values from -0.1875 to 0.1875
- w_x: bfloat16 [1024, 2048], P('dp', 'tensor'), may hold values from -0.1875 to 0.1875
- w_bc: bfloat16 [1024, 256], P('dp'), may hold values from -0.1875 to 0.1875
- w_dt: bfloat16 [1024, 32], P('dp', 'tensor'), may hold values from -0.1875 to 0.1875
- w_out: bfloat16 [2048, 1024], P('tensor', 'dp'), may hold values from -0.125 to 0.125
- norm_gain: bfloat16 [1024], P('dp'), may hold values from 0.5 to 1.5
- conv_x: bfloat16 [4, 32, 64], P(None, 'tensor', 'dp'), may hold values from -3 to 3
- bias_x: bfloat16 [32, 64], P('tensor', 'dp'), may hold values from -2 to 2
- conv_bc: bfloat16 [4, 256], P(None, 'dp'), may hold values from -3 to 3
- bias_bc: bfloat16 [256], P('dp'), may hold values from -2 to 2
- gate_gain: bfloat16 [32, 64], P('tensor', 'dp'), may hold values from 0.5 to 1.5
- dt_bias: float32 [32], P('tensor'), may hold values from -6.9 to -2.3
- a_log: float32 [32], P('tensor'), may hold values from 0 to 2.77
- d_skip: float32 [32], P('tensor'), may hold values from 0.5 to 1.5
Outputs:
- block_out: bfloat16 [24576, 1024], P(('dp', 'tensor'))
- grad_hidden: float32 [24576, 1024], P(('dp', 'tensor'))
- grad_w_z: float32 [1024, 2048], P('dp', 'tensor')
- grad_w_x: float32 [1024, 2048], P('dp', 'tensor')
- grad_w_bc: float32 [1024, 256], P('dp')
- grad_w_dt: float32 [1024, 32], P('dp', 'tensor')
- grad_w_out: float32 [2048, 1024], P('tensor', 'dp')
- grad_norm_gain: float32 [1024], P('dp')
- grad_conv_x: float32 [4, 32, 64], P(None, 'tensor', 'dp')
- grad_bias_x: float32 [32, 64], P('tensor', 'dp')
- grad_conv_bc: float32 [4, 256], P(None, 'dp')
- grad_bias_bc: float32 [256], P('dp')
- grad_gate_gain: float32 [32, 64], P('tensor', 'dp')
- grad_dt_bias: float32 [32], P('tensor')
- grad_a_log: float32 [32], P('tensor')
- grad_d_skip: float32 [32], P('tensor')
The draws below stay inside these ranges and needn't reach their ends.
Inputs may be any that keep to these rules, and one draw needn't show every extreme that they name: `segments`: segment numbers never fall along the tokens; a document holds 1 to 800 tokens and one holds exactly 800.
All inputs are finite; a program needn't handle non-finite values.
Results may differ from the reference program's by a relative error of at most 0.0085.
Values may be sent and summed in bfloat16 or wider, within the bound.
A program may use at most 192 MiB of HBM per device.

```python
import math
import jax
import jax.numpy as jnp
import numpy as np
from jax import lax

D = 1024
H = 32
P_SIZE = 64
N = 128
CONV = 4
BLOCK = 256
SEQ_LEN = 1024
MOST_DOC = 800
DI = 2048
TOKENS = 24576


def block_scale(stream_key, extent, cuts, least, largest):
    def one(position, parts):
        heights = jax.random.uniform(jax.random.fold_in(jax.random.fold_in(stream_key, 6), position), (parts,), jnp.float32, least / len(cuts), largest / len(cuts))
        return jnp.repeat(jnp.exp(heights), extent[position] // parts).reshape((-1,) + (1,) * (len(extent) - position - 1))

    loudness = one(*cuts[0])
    for cut in cuts[1:]:
        loudness = loudness * one(*cut)
    return loudness


def length_profile(number_of, total, reach, slope):
    portions = [(1 << 20) // math.isqrt(standing ** slope) + 1 for standing in range(2, number_of + 1)]
    spare, counts = total - reach - (number_of - 1), [1] * (number_of - 1)
    while spare > 0:
        free = [i for i in range(number_of - 1) if counts[i] < reach]
        whole, remaining = sum([portions[i] for i in free]), spare
        for i in free:
            more = min(reach - counts[i], max(1, remaining * portions[i] // whole), spare)
            counts[i] = counts[i] + more
            spare = spare - more
    return np.array([reach] + counts)


def uneven_parts(stream_key, number_of, total, bound, lean):
    if number_of == 2:
        one = jax.random.randint(stream_key, (), max(1, total - bound), min(bound, total - 1) + 1)
        return jnp.stack([one, total - one])
    sizes = jnp.asarray(length_profile(number_of, total, bound, lean), jnp.int32)
    pairs = (number_of - 1) // 2
    giver, taker = sizes[1:1 + 2 * pairs:2], sizes[2:2 + 2 * pairs:2]
    margin = jnp.minimum(giver - 1, bound - taker)
    passed = jax.random.randint(jax.random.fold_in(stream_key, 1), (pairs,), 0, 1 << 20) % (margin + 1)
    sizes = sizes.at[1:1 + 2 * pairs:2].set(giver - passed).at[2:2 + 2 * pairs:2].set(taker + passed)
    return sizes[jax.random.permutation(jax.random.fold_in(stream_key, 2), number_of)]


def normal_values(rng, extent, width, reach, split=(), kind=jnp.bfloat16):
    drawn = jax.random.normal(rng, extent, jnp.float32) * width
    if len(split) > 0:
        drawn = block_scale(rng, extent, split, -0.22, 0.18) * drawn
    return jnp.clip(drawn, min=-reach, max=reach).astype(kind)


def setup_inputs(seed: int = 0) -> dict:
    arg_keys = jax.random.split(jax.random.key(seed), 18)
    return {
        "hidden_in": normal_values(arg_keys[0], (TOKENS, D), 1.0, 6.0, ((0, 32),)),
        "segments": jnp.searchsorted(jnp.cumsum(uneven_parts(arg_keys[1], TOKENS // (3 * MOST_DOC // 8), TOKENS, MOST_DOC, 0)), jnp.arange(TOKENS), side="right").astype(jnp.int32),
        "cotangent": normal_values(arg_keys[2], (TOKENS, D), 1.0, 6.0, ((0, 32),)),
        "w_z": normal_values(arg_keys[3], (D, DI), D ** -0.5, 0.1875, ((0, 8), (1, 4))),
        "w_x": normal_values(arg_keys[4], (D, DI), D ** -0.5, 0.1875, ((0, 8), (1, 4))),
        "w_bc": normal_values(arg_keys[5], (D, 2 * N), D ** -0.5, 0.1875, ((0, 8),)),
        "w_dt": normal_values(arg_keys[6], (D, H), D ** -0.5, 0.1875, ((0, 8), (1, 4))),
        "w_out": normal_values(arg_keys[7], (DI, D), DI ** -0.5, 0.125, ((0, 4), (1, 8))),
        "norm_gain": jnp.clip(1.0 + 0.1 * jax.random.normal(arg_keys[8], (D,), jnp.float32), 0.5, 1.5).astype(jnp.bfloat16),
        "conv_x": normal_values(arg_keys[9], (CONV, H, P_SIZE), CONV ** -0.5, 3.0, ((1, 4), (2, 8))),
        "bias_x": normal_values(arg_keys[10], (H, P_SIZE), 0.3, 2.0, ((0, 4), (1, 8))),
        "conv_bc": normal_values(arg_keys[11], (CONV, 2 * N), CONV ** -0.5, 3.0, ((1, 8),)),
        "bias_bc": normal_values(arg_keys[12], (2 * N,), 0.3, 2.0, ((0, 8),)),
        "gate_gain": jnp.clip(1.0 + 0.1 * jax.random.normal(arg_keys[13], (H, P_SIZE), jnp.float32), 0.5, 1.5).astype(jnp.bfloat16),
        "dt_bias": jnp.clip(-6.9 + 4.6000001430511475 * jax.random.uniform(arg_keys[14], (H,), jnp.float32) ** block_scale(arg_keys[14], (H,), ((0, 4),), -0.2, 0.2), -6.9, -2.3),
        "a_log": jnp.clip(2.77 * jax.random.uniform(arg_keys[15], (H,), jnp.float32) ** block_scale(arg_keys[15], (H,), ((0, 4),), -0.2, 0.2), 0.0, 2.77),
        "d_skip": jnp.clip(0.5 + 1.0 * jax.random.uniform(arg_keys[16], (H,), jnp.float32) ** block_scale(arg_keys[16], (H,), ((0, 4),), -0.2, 0.2), 0.5, 1.5),
    }


EPSILON = 1e-05
HIGHEST = lax.Precision.HIGHEST

@jax.custom_vjp
def low(v):
    return lax.optimization_barrier(v.astype(jnp.bfloat16)).astype(jnp.float32)

@jax.custom_vjp
def low_back(v):
    return v

def low_keep(v):
    return (low(v), None)

def low_pass(kept, grad):
    return (grad,)

def back_keep(v):
    return (v, None)

def back_low(kept, grad):
    return (low(grad),)
low.defvjp(low_keep, low_pass)
low_back.defvjp(back_keep, back_low)

def causal_conv(inputs, filters, shifts, doc_rows):
    tap_count = filters.shape[0]
    summed = shifts + filters[tap_count - 1] * inputs
    for offset in range(1, tap_count):
        shifted = jnp.pad(inputs, ((0, 0), (offset, 0), (0, 0)))[:, :-offset]
        shifted_doc = jnp.pad(doc_rows, ((0, 0), (offset, 0)), constant_values=-1)[:, :-offset]
        same_doc = (shifted_doc == doc_rows).astype(inputs.dtype)
        summed = summed + filters[tap_count - 1 - offset] * shifted * same_doc[:, :, None]
    return summed

def scan_sequence(values, b_rows, c_rows, step_sizes, decay_rates, skip_gain, doc_ids, block_len):
    length, head_count, head_width = values.shape
    blocks_count = length // block_len
    value_blocks = values.reshape(blocks_count, block_len, head_count, head_width)
    b_blocks = b_rows.reshape(blocks_count, block_len, -1)
    c_blocks = c_rows.reshape(blocks_count, block_len, -1)
    step_blocks = jnp.transpose(step_sizes.reshape(blocks_count, block_len, head_count), (0, 2, 1))
    doc_blocks = doc_ids.reshape(blocks_count, block_len)
    cumulative = jnp.cumsum(step_blocks * decay_rates[None, :, None], axis=2)
    positions = jnp.arange(block_len)
    causal = positions[:, None] >= positions[None, :]
    same_doc = (doc_blocks[:, :, None] == doc_blocks[:, None, :]) & causal[None]
    mask_float = same_doc.astype(values.dtype)[:, None]
    spread = cumulative[:, :, :, None] - cumulative[:, :, None, :]
    decays = jnp.exp(spread * mask_float) * mask_float
    scores = jnp.einsum('ctn,csn->cts', c_blocks, b_blocks, precision=HIGHEST)
    weights = decays * scores[:, None] * step_blocks[:, :, None, :]
    intra_out = jnp.einsum('chts,cshp->cthp', weights, value_blocks, precision=HIGHEST)
    last_doc = doc_blocks[:, -1]
    tail_mask = (doc_blocks == last_doc[:, None]).astype(values.dtype)
    to_end = jnp.exp(cumulative[:, :, -1:] - cumulative) * tail_mask[:, None, :] * step_blocks
    local_states = jnp.einsum('csn,chs,cshp->chnp', b_blocks, to_end, value_blocks, precision=HIGHEST)
    carry_state = local_states[0]
    pieces = [intra_out[0]]
    for block_index in range(1, blocks_count):
        reach_mask = (doc_blocks[block_index] == last_doc[block_index - 1]).astype(values.dtype)
        entry_decay = jnp.exp(cumulative[block_index]) * reach_mask[None, :]
        carried = jnp.einsum('tn,hnp->thp', c_blocks[block_index], carry_state, precision=HIGHEST)
        pieces.append(intra_out[block_index] + carried * jnp.transpose(entry_decay)[:, :, None])
        keep_state = (last_doc[block_index] == last_doc[block_index - 1]).astype(values.dtype)
        carry_state = local_states[block_index] + (keep_state * jnp.exp(cumulative[block_index, :, -1]))[:, None, None] * carry_state
    result = jnp.stack(pieces).reshape(length, head_count, head_width)
    return result + skip_gain[None, :, None] * values

def mixer(proj_x, proj_bc, proj_dt, conv_x, bias_x, conv_bc, bias_bc, dt_bias, a_log, d_skip, doc_ids, seq_len, block_len):
    tokens_count = proj_x.shape[0]
    seq_count = tokens_count // seq_len
    head_count = proj_dt.shape[1]
    head_width = proj_x.shape[1] // head_count
    state_size = proj_bc.shape[1] // 2
    doc_rows = doc_ids.reshape(seq_count, seq_len)
    filter_x = conv_x.reshape(conv_x.shape[0], -1)
    x_conv = jax.nn.silu(causal_conv(proj_x.reshape(seq_count, seq_len, -1), filter_x, bias_x.reshape(-1), doc_rows))
    bc_conv = jax.nn.silu(causal_conv(proj_bc.reshape(seq_count, seq_len, -1), conv_bc, bias_bc, doc_rows))
    step_sizes = jax.nn.softplus(proj_dt + dt_bias).reshape(seq_count, seq_len, head_count)
    decay_rates = -jnp.exp(a_log)

    def one_sequence(seq_item):
        x_seq, bc_seq, dt_seq, doc_seq = seq_item
        out_seq = scan_sequence(x_seq.reshape(seq_len, head_count, head_width), bc_seq[:, :state_size], bc_seq[:, state_size:], dt_seq, decay_rates, d_skip, doc_seq, block_len)
        return out_seq.reshape(seq_len, head_count * head_width)
    mixed = lax.map(jax.checkpoint(one_sequence), (x_conv, bc_conv, step_sizes, doc_rows))
    return mixed.reshape(tokens_count, head_count * head_width)

def reference(hidden_in, segments, cotangent, w_z, w_x, w_bc, w_dt, w_out, norm_gain, conv_x, bias_x, conv_bc, bias_bc, gate_gain, dt_bias, a_log, d_skip):
    floats = tuple((v.astype(jnp.float32) for v in (hidden_in, w_z, w_x, w_bc, w_dt, w_out, norm_gain, conv_x, bias_x, conv_bc, bias_bc, gate_gain, dt_bias, a_log, d_skip)))

    def forward(resid, proj_z, proj_x, proj_bc, proj_dt, proj_out, gain_in, filter_x, shift_x, filter_bc, shift_bc, gain_gate, dt_shift, log_rate, skip_gain):
        inv_in = lax.rsqrt(lax.optimization_barrier(jnp.mean(resid * resid, -1, keepdims=True)) + EPSILON)
        normed = low(resid * inv_in * gain_in)
        gate_raw = low_back(jnp.dot(normed, proj_z, precision=HIGHEST))
        value_raw = low_back(jnp.dot(normed, proj_x, precision=HIGHEST))
        bc_raw = low_back(jnp.dot(normed, proj_bc, precision=HIGHEST))
        dt_raw = low_back(jnp.dot(normed, proj_dt, precision=HIGHEST))
        mixed = mixer(value_raw, bc_raw, dt_raw, filter_x, shift_x, filter_bc, shift_bc, dt_shift, log_rate, skip_gain, segments, SEQ_LEN, BLOCK)
        gated = mixed * jax.nn.silu(gate_raw)
        inv_gate = lax.rsqrt(lax.optimization_barrier(jnp.mean(gated * gated, -1, keepdims=True)) + EPSILON)
        scaled = low(gated * inv_gate * gain_gate.reshape(-1))
        return resid + jnp.dot(scaled, proj_out, precision=HIGHEST)
    result, pullback = jax.vjp(forward, *floats)
    grads = pullback(cotangent.astype(jnp.float32))
    return (result.astype(jnp.bfloat16), grads[0], grads[1], grads[2], grads[3], grads[4], grads[5], grads[6], grads[7], grads[8], grads[9], grads[10], grads[11], grads[12], grads[13], grads[14])
```

```python
import functools

import jax
import jax.numpy as jnp
from jax import lax
from jax.experimental import pallas as pl
from jax.experimental.pallas import tpu as pltpu
from jax.sharding import PartitionSpec as P

SEQ_LEN = 1024
EPSILON = 1e-05
T = 128
F32 = jnp.float32
BF16 = jnp.bfloat16


def mm(a, b):
    return lax.dot_general(a, b, (((1,), (0,)), ((), ())), preferred_element_type=F32)


def mm_nt(a, b):
    return lax.dot_general(a, b, (((1,), (1,)), ((), ())), preferred_element_type=F32)


def mm_tn(a, b):
    return lax.dot_general(a, b, (((0,), (0,)), ((), ())), preferred_element_type=F32)


def split2(v):
    hi = v.astype(BF16)
    return hi, (v - hi.astype(F32)).astype(BF16)


def split3(v):
    hi = v.astype(BF16)
    rest = v - hi.astype(F32)
    mid = rest.astype(BF16)
    return hi, mid, (rest - mid.astype(F32)).astype(BF16)


def sigmoid(v):
    return 1.0 / (1.0 + jnp.exp(-v))


def softplus(v):
    return jnp.maximum(v, 0.0) + jnp.log(1.0 + jnp.exp(-jnp.abs(v)))


def expand(v, spread):
    hi, lo = split2(v)
    return mm(hi, spread) + mm(lo, spread)


def per_head(v, spread):
    hi, lo = split2(v)
    return mm_nt(hi, spread) + mm_nt(lo, spread)


def decay_parts(dt_raw, dt_bias, rate, aux, spread):
    steps = softplus(dt_raw + dt_bias)
    rows = lax.broadcasted_iota(jnp.int32, (T, T), 0)
    cols = lax.broadcasted_iota(jnp.int32, (T, T), 1)
    tri = (rows >= cols).astype(BF16)
    p0, p1, p2 = split3(steps * rate)
    cum = mm(tri, p0) + mm(tri, p1) + mm(tri, p2)
    reach, tail = aux[:, 1:2], aux[:, 2:3]
    entry = jnp.exp(cum) * reach
    to_end = jnp.exp(cum[T - 1 : T] - cum) * tail
    wide = expand(jnp.concatenate([steps, entry, to_end], 0), spread)
    return steps, cum, tri, wide[:T], wide[T : 2 * T], wide[2 * T :], rows >= cols


def decay_of(cum, cum_t, mask, h):
    return jnp.exp(jnp.where(mask, cum[:, h : h + 1] - cum_t[h : h + 1, :], -1e30))


def halves(v):
    low = lax.broadcasted_iota(jnp.int32, v.shape, 1) < v.shape[1] // 2
    zero = jnp.zeros_like(v)
    return jnp.where(low, v, zero), jnp.where(low, zero, v)


def forward_kernel(
    heads, di, ns,
    proj_ref, dyn_ref, aux_ref, seg_ref, filt_ref, bias_ref, head_ref, chan_ref, spread_ref,
    pre_ref, y_ref, v_ref, state_out_ref, stats_ref,
    ext, state,
):
    @pl.when(pl.program_id(0) == 0)
    def _():
        ext[...] = jnp.zeros_like(ext)
        state[...] = jnp.zeros_like(state)

    aux = aux_ref[...]
    spread = spread_ref[...]
    raw = proj_ref[:, di : 2 * di + 2 * ns]
    ext[8:, :] = raw
    filt = filt_ref[...]
    pre = bias_ref[...] + filt[3:4] * raw
    for k in range(1, 4):
        pre = pre + filt[3 - k : 4 - k] * (ext[8 - k : 8 - k + T, :] * aux[:, 2 + k : 3 + k])
    ext[0:8, :] = ext[T : T + 8, :]
    pre_ref[...] = pre
    act = pre * sigmoid(pre)
    xc = act[:, :di]
    b_low = act[:, di : di + ns].astype(BF16)
    c_low = act[:, di + ns :].astype(BF16)
    dt_raw = proj_ref[:, 2 * di + 2 * ns :]
    steps, cum, tri, dt_e, entry_e, end_e, causal = decay_parts(
        dt_raw, head_ref[0:1], head_ref[1:2], aux, spread
    )
    cum_t = cum.T
    mask = causal & (aux[:, 0:1] == seg_ref[0])
    xdt = xc * dt_e
    xdt_low = xdt.astype(BF16)
    scores = mm_nt(c_low, b_low)
    pieces = []
    for j in range(heads // 2):
        pair = xdt_low[:, 128 * j : 128 * (j + 1)]
        xa, xb = halves(pair)
        ma = (decay_of(cum, cum_t, mask, 2 * j) * scores).astype(BF16)
        mb = (decay_of(cum, cum_t, mask, 2 * j + 1) * scores).astype(BF16)
        pieces.append(mm(jnp.concatenate([ma, mb], 1), jnp.concatenate([xa, xb], 0)))
    state_low = state[...].astype(BF16)
    state_out_ref[0] = state_low
    chan = chan_ref[...]
    y = (
        jnp.concatenate(pieces, 1)
        + entry_e * mm(c_low, state_low)
        + chan[0:1] * xc
    )
    state[...] = entry_e[T - 1 : T] * state[...] + mm_tn(b_low, (end_e * xdt).astype(BF16))
    y_ref[...] = y
    z = proj_ref[:, :di]
    u = y * z * sigmoid(z)
    v = u * chan[1:2]
    v_ref[...] = v.astype(BF16)
    ones = jnp.ones((8, di), BF16)
    s_hi, s_lo = split2(u * u)
    i_hi, i_lo = split2(v * dyn_ref[...])
    square = mm_nt(ones, s_hi) + mm_nt(ones, s_lo)
    inner = mm_nt(ones, i_hi) + mm_nt(ones, i_lo)
    upper = lax.broadcasted_iota(jnp.int32, (8, T), 0) < 4
    stats_ref[0] = jnp.where(upper, square, inner)


def backward_kernel(
    heads, di, ns,
    proj_ref, dyn_ref, pre_ref, y_ref, state_ref, aux_ref, aux2_ref, seg_ref,
    filt_ref, head_ref, chan_ref, spread_ref,
    d_ref, conv_acc, chan_acc, head_acc,
    ext, d_state,
):
    @pl.when(pl.program_id(0) == 0)
    def _():
        ext[...] = jnp.zeros_like(ext)
        d_state[...] = jnp.zeros_like(d_state)
        conv_acc[...] = jnp.zeros_like(conv_acc)
        chan_acc[...] = jnp.zeros_like(chan_acc)
        head_acc[...] = jnp.zeros_like(head_acc)

    aux = aux_ref[...]
    spread = spread_ref[...]
    chan = chan_ref[...]
    skip, gain = chan[0:1], chan[1:2]
    inv, slope = aux2_ref[:, 0:1], aux2_ref[:, 1:2]
    y = y_ref[...]
    dyn = dyn_ref[...]
    z = proj_ref[:, :di]
    sig_z = sigmoid(z)
    silu_z = z * sig_z
    u = y * silu_z
    d_u = inv * gain * dyn - u * slope
    d_ref[:, :di] = (d_u * y * sig_z * (1.0 + z * (1.0 - sig_z))).astype(BF16)
    chan_acc[0:1, :] += jnp.sum(dyn * u * inv, 0, keepdims=True)
    dy = d_u * silu_z
    dy_low = dy.astype(BF16)
    dy_r = dy_low.astype(F32)

    pre = pre_ref[...]
    sig = sigmoid(pre)
    act = pre * sig
    d_act = sig * (1.0 + pre * (1.0 - sig))
    xc = act[:, :di]
    b_low = act[:, di : di + ns].astype(BF16)
    c_low = act[:, di + ns :].astype(BF16)
    rate = head_ref[1:2]
    dt_in = proj_ref[:, 2 * di + 2 * ns :] + head_ref[0:1]
    steps, cum, tri, dt_e, entry_e, end_e, causal = decay_parts(
        proj_ref[:, 2 * di + 2 * ns :], head_ref[0:1], rate, aux, spread
    )
    cum_t = cum.T
    mask = causal & (aux[:, 0:1] == seg_ref[0])
    xdt = xc * dt_e
    xdt_low = xdt.astype(BF16)
    xend_low = (end_e * xdt).astype(BF16)
    scores = mm_nt(c_low, b_low)
    d_scores = jnp.zeros((T, T), F32)
    pieces = []
    for j in range(heads // 2):
        lanes = slice(128 * j, 128 * (j + 1))
        xa, xb = halves(xdt_low[:, lanes])
        dya, dyb = halves(dy_low[:, lanes])
        la = decay_of(cum, cum_t, mask, 2 * j)
        lb = decay_of(cum, cum_t, mask, 2 * j + 1)
        ma = (la * scores).astype(BF16)
        mb = (lb * scores).astype(BF16)
        dm = mm_nt(dy_low[:, lanes], jnp.concatenate([xa, xb], 0))
        d_scores = d_scores + la * dm[:, :T] + lb * dm[:, T:]
        pieces.append(mm_tn(jnp.concatenate([ma, mb], 0), jnp.concatenate([dya, dyb], 0)))
    dx_intra = jnp.concatenate(pieces, 1)
    s_in = state_ref[0]
    ds_low = d_state[...].astype(BF16)
    dx_end = mm(b_low, ds_low)
    ey_low = (entry_e * dy_r).astype(BF16)
    ds_scores = d_scores.astype(BF16)
    d_c = mm(ds_scores, b_low) + mm_nt(ey_low, s_in)
    d_b = mm_tn(ds_scores, c_low) + mm_nt(xend_low, ds_low)
    d_xdt = dx_intra + end_e * dx_end
    d_xc = dt_e * d_xdt + skip * dy
    chan_acc[1:2, :] += jnp.sum(dy * xc, 0, keepdims=True)
    ended = xend_low.astype(F32) * dx_end
    keep_e = entry_e[T - 1 : T]
    total = jnp.sum(ended, 0, keepdims=True) + keep_e * jnp.sum(
        d_state[...] * s_in.astype(F32), 0, keepdims=True
    )
    last = lax.broadcasted_iota(jnp.int32, (T, 1), 0) == T - 1
    flow = dy_r * (y - skip * xc) - xdt_low.astype(F32) * dx_intra - ended
    flow = flow + jnp.where(last, total, 0.0)
    d_state[...] = keep_e * d_state[...] + mm_tn(c_low, ey_low)
    sums = per_head(jnp.concatenate([flow, d_xdt * xc], 0), spread)
    q0, q1, q2 = split3(sums[:T])
    d_log = mm_tn(tri, q0) + mm_tn(tri, q1) + mm_tn(tri, q2)
    d_dt = (sums[T:] + rate * d_log) * sigmoid(dt_in)
    d_ref[:, 2 * di + 2 * ns :] = d_dt.astype(BF16)
    head_acc[0:1, :] += jnp.sum(d_dt, 0, keepdims=True)
    head_acc[1:2, :] += jnp.sum(d_log * steps, 0, keepdims=True)

    d_pre = jnp.concatenate([d_xc, d_b, d_c], 1) * d_act
    ext[0:T, :] = d_pre
    raw = proj_ref[:, di : 2 * di + 2 * ns]
    filt = filt_ref[...]
    d_raw = filt[3:4] * d_pre
    conv_acc[3:4, :] += jnp.sum(raw * d_pre, 0, keepdims=True)
    conv_acc[4:5, :] += jnp.sum(d_pre, 0, keepdims=True)
    for k in range(1, 4):
        moved = ext[k : k + T, :] * aux[:, 5 + k : 6 + k]
        d_raw = d_raw + filt[3 - k : 4 - k] * moved
        conv_acc[3 - k : 4 - k, :] += jnp.sum(raw * moved, 0, keepdims=True)
    ext[T : T + 8, :] = ext[0:8, :]
    d_ref[:, di : 2 * di + 2 * ns] = d_raw.astype(BF16)


def whole(shape):
    return pl.BlockSpec(shape, lambda i: (0,) * len(shape))


def run_forward(heads, di, ns, proj, dyn, aux, seg_rows, filt, bias, head, chan, spread):
    tokens, width = proj.shape
    count = tokens // T
    conv = di + 2 * ns
    row = lambda w: pl.BlockSpec((T, w), lambda i: (i, 0))
    return pl.pallas_call(
        functools.partial(forward_kernel, heads, di, ns),
        grid=(count,),
        in_specs=[
            row(width), row(di), row(16),
            pl.BlockSpec((1, 1, T), lambda i: (i, 0, 0)),
            whole(filt.shape), whole(bias.shape), whole(head.shape),
            whole(chan.shape), whole(spread.shape),
        ],
        out_specs=[
            row(conv), row(di), row(di),
            pl.BlockSpec((1, ns, di), lambda i: (i, 0, 0)),
            pl.BlockSpec((1, 8, T), lambda i: (i, 0, 0)),
        ],
        out_shape=[
            jax.ShapeDtypeStruct((tokens, conv), F32),
            jax.ShapeDtypeStruct((tokens, di), F32),
            jax.ShapeDtypeStruct((tokens, di), BF16),
            jax.ShapeDtypeStruct((count, ns, di), BF16),
            jax.ShapeDtypeStruct((count, 8, T), F32),
        ],
        scratch_shapes=[pltpu.VMEM((T + 8, conv), F32), pltpu.VMEM((ns, di), F32)],
        compiler_params=pltpu.CompilerParams(vmem_limit_bytes=40 * 1024 * 1024),
        cost_estimate=pl.CostEstimate(
            flops=2 * tokens * di * 1024, bytes_accessed=tokens * 4 * 4000, transcendentals=tokens * 3000
        ),
    )(proj, dyn, aux, seg_rows, filt, bias, head, chan, spread)


def run_backward(
    heads, di, ns, proj, dyn, pre, y, states, aux, aux2, seg_rows, filt, head, chan, spread
):
    tokens, width = proj.shape
    count = tokens // T
    conv = di + 2 * ns
    row = lambda w: pl.BlockSpec((T, w), lambda i: (count - 1 - i, 0))
    return pl.pallas_call(
        functools.partial(backward_kernel, heads, di, ns),
        grid=(count,),
        in_specs=[
            row(width), row(di), row(conv), row(di),
            pl.BlockSpec((1, ns, di), lambda i: (count - 1 - i, 0, 0)),
            row(16), row(2),
            pl.BlockSpec((1, 1, T), lambda i: (count - 1 - i, 0, 0)),
            whole(filt.shape), whole(head.shape), whole(chan.shape), whole(spread.shape),
        ],
        out_specs=[row(width), whole((8, conv)), whole((8, di)), whole((8, 128))],
        out_shape=[
            jax.ShapeDtypeStruct((tokens, width), BF16),
            jax.ShapeDtypeStruct((8, conv), F32),
            jax.ShapeDtypeStruct((8, di), F32),
            jax.ShapeDtypeStruct((8, 128), F32),
        ],
        scratch_shapes=[pltpu.VMEM((T + 8, conv), F32), pltpu.VMEM((ns, di), F32)],
        compiler_params=pltpu.CompilerParams(vmem_limit_bytes=40 * 1024 * 1024),
        cost_estimate=pl.CostEstimate(
            flops=4 * tokens * di * 1024, bytes_accessed=tokens * 4 * 4000, transcendentals=tokens * 4000
        ),
    )(proj, dyn, pre, y, states, aux, aux2, seg_rows, filt, head, chan, spread)


def token_masks(segments):
    seg = segments.reshape(-1, SEQ_LEN)
    count, length = seg.shape
    blocks = seg.reshape(count, length // T, T)
    last = blocks[:, :, -1:]
    before = jnp.pad(last, ((0, 0), (1, 0), (0, 0)), constant_values=-1)[:, :-1]
    columns = [seg, (blocks == before).reshape(seg.shape), (blocks == last).reshape(seg.shape)]
    for k in range(1, 4):
        moved = jnp.pad(seg, ((0, 0), (k, 0)), constant_values=-1)[:, :-k]
        columns.append(moved == seg)
    for k in range(1, 4):
        moved = jnp.pad(seg, ((0, 0), (0, k)), constant_values=-1)[:, k:]
        columns.append(moved == seg)
    columns = [c.astype(F32).reshape(-1) for c in columns]
    columns += [jnp.zeros_like(columns[0])] * (16 - len(columns))
    return jnp.stack(columns, 1), seg.astype(F32).reshape(-1, 1, T)


def shards(
    hidden_in, segments, cotangent, w_z, w_x, w_bc, w_dt, w_out, norm_gain,
    conv_x, bias_x, conv_bc, bias_bc, gate_gain, dt_bias, a_log, d_skip,
):
    dp = lax.axis_size("dp")
    tp = lax.axis_size("tensor")
    own_rows, width = hidden_in.shape
    di = w_z.shape[1]
    heads = w_dt.shape[1]
    ns = w_bc.shape[1] // 2
    per = di // heads
    shard = w_z.shape[0]
    channels = di * tp

    hidden_all = lax.all_gather(hidden_in, "tensor", axis=0, tiled=True)
    small_parts = [norm_gain, conv_x, bias_x, conv_bc, bias_bc, gate_gain]
    small = lax.all_gather(jnp.concatenate([p.reshape(-1) for p in small_parts]), "dp")
    w_local = jnp.concatenate(
        [w_z, w_x, w_bc, w_dt, jnp.zeros((shard, 128 - heads), BF16), w_out.T], 1
    )
    w_full = lax.all_gather(w_local, "dp", axis=0, tiled=True)
    cot_all = lax.all_gather(cotangent, "tensor", axis=0, tiled=True)
    in_width = 2 * di + 2 * ns + 128
    w_in = w_full[:, :in_width]
    w_out_t = w_full[:, in_width:]
    out_all = lax.all_gather(w_out_t, "tensor", axis=0)

    small = small.astype(F32)
    fields, at = [], 0
    for p in small_parts:
        fields.append(small[:, at : at + p.size].reshape((dp,) + p.shape))
        at += p.size
    gain_in = fields[0].reshape(-1)
    filter_x = jnp.transpose(fields[1], (1, 2, 0, 3)).reshape(4, di)
    shift_x = jnp.transpose(fields[2], (1, 0, 2)).reshape(1, di)
    filter_bc = jnp.transpose(fields[3], (1, 0, 2)).reshape(4, 2 * ns)
    shift_bc = fields[4].reshape(1, 2 * ns)
    gain_gate = jnp.transpose(fields[5], (1, 0, 2)).reshape(1, di)
    filt = jnp.concatenate([filter_x, filter_bc], 1)
    bias = jnp.concatenate([shift_x, shift_bc], 1)
    rate = -jnp.exp(a_log)
    head = jnp.pad(jnp.stack([dt_bias, rate]), ((0, 6), (0, 128 - heads)))
    chan = jnp.concatenate([jnp.repeat(d_skip, per)[None], gain_gate, jnp.zeros((6, di), F32)], 0)
    spread = (jnp.arange(128)[:, None] == jnp.arange(di)[None, :] // per).astype(BF16)
    aux, seg_rows = token_masks(segments)

    full = hidden_all.astype(F32)
    inv_full = lax.rsqrt(jnp.mean(full * full, -1, keepdims=True) + EPSILON)
    normed = (full * inv_full * gain_in).astype(BF16)
    proj = mm(normed, w_in)
    dyn = mm(cot_all, w_out_t)
    pre, y, v_low, states, stats = run_forward(
        heads, di, ns, proj, dyn, aux, seg_rows, filt, bias, head, chan, spread
    )
    v_own = lax.all_to_all(v_low, "tensor", split_axis=0, concat_axis=1, tiled=True)
    sums = lax.psum(jnp.stack([stats[:, 0].reshape(-1), stats[:, 4].reshape(-1)]), "tensor")
    inv_gate = lax.rsqrt(sums[0] / channels + EPSILON)
    slope = inv_gate * inv_gate * inv_gate * sums[1] / channels
    aux2 = jnp.stack([inv_gate, slope], 1)
    d_all, conv_acc, chan_acc, head_acc = run_backward(
        heads, di, ns, proj, dyn, pre, y, states, aux, aux2, seg_rows, filt, head, chan, spread
    )
    resid = hidden_in.astype(F32)
    me = lax.axis_index("tensor")
    inv_own = lax.dynamic_slice_in_dim(inv_gate, me * own_rows, own_rows)[:, None]
    out_rows = sum(mm_nt(v_own[:, r * di : (r + 1) * di], out_all[r]) for r in range(tp))
    block_out = (resid + inv_own * out_rows).astype(BF16)

    scaled = (v_low.astype(F32) * inv_gate[:, None]).astype(BF16)
    grad_out = lax.psum_scatter(mm_tn(cot_all, scaled), "dp", scatter_dimension=0, tiled=True)
    d_part = mm_nt(d_all, w_in)
    d_rows = lax.psum_scatter(d_part, "tensor", scatter_dimension=0, tiled=True)
    grad_in = lax.psum_scatter(mm_tn(normed, d_all), "dp", scatter_dimension=0, tiled=True)

    inv_in = lax.rsqrt(jnp.mean(resid * resid, -1, keepdims=True) + EPSILON)
    grad_gain_part = jnp.sum(d_rows * resid * inv_in, 0)
    weighted = d_rows * gain_in
    grad_hidden = (
        cotangent.astype(F32)
        + inv_in * weighted
        - resid * inv_in**3 * jnp.mean(weighted * resid, -1, keepdims=True)
    )

    def by_owner(value, axis):
        shape = value.shape
        cut = value.reshape(shape[:axis] + (dp, shape[axis] // dp) + shape[axis + 1 :])
        return jnp.moveaxis(cut, axis, 0).reshape(dp, -1)

    head_part = jnp.concatenate(
        [
            head_acc[0, :heads],
            rate * head_acc[1, :heads],
            jnp.sum(chan_acc[1].reshape(heads, per), 1),
        ]
    )
    packed = jnp.concatenate(
        [
            by_owner(grad_gain_part, 0),
            by_owner(conv_acc[:4, di:], 1),
            by_owner(conv_acc[4, di:], 0),
            by_owner(conv_acc[:4, :di].reshape(4, heads, per), 2),
            by_owner(conv_acc[4, :di].reshape(heads, per), 1),
            by_owner(chan_acc[0].reshape(heads, per), 1),
            jnp.broadcast_to(head_part[None], (dp, 3 * heads)),
        ],
        1,
    )
    mine = lax.psum_scatter(packed, "dp", scatter_dimension=0, tiled=True).reshape(-1)
    n_gain, n_conv, n_bias = width // dp, 4 * 2 * ns // dp, 2 * ns // dp
    n_shared = n_gain + n_conv + n_bias
    shared = lax.psum(
        jnp.concatenate([grad_in[:, 2 * di : 2 * di + 2 * ns].reshape(-1), mine[:n_shared]]), "tensor"
    )
    n_bc = shard * 2 * ns
    rest = mine[n_shared:]
    n_x = 4 * di // dp
    n_c = di // dp
    return (
        block_out,
        grad_hidden,
        grad_in[:, :di],
        grad_in[:, di : 2 * di],
        shared[:n_bc].reshape(shard, 2 * ns),
        grad_in[:, 2 * di + 2 * ns : 2 * di + 2 * ns + heads],
        grad_out.T,
        shared[n_bc : n_bc + n_gain],
        rest[:n_x].reshape(4, heads, per // dp),
        rest[n_x : n_x + n_c].reshape(heads, per // dp),
        shared[n_bc + n_gain : n_bc + n_gain + n_conv].reshape(4, n_bias),
        shared[n_bc + n_gain + n_conv :],
        rest[n_x + n_c : n_x + 2 * n_c].reshape(heads, per // dp),
        rest[n_x + 2 * n_c : n_x + 2 * n_c + heads],
        rest[n_x + 2 * n_c + heads : n_x + 2 * n_c + 2 * heads],
        rest[n_x + 2 * n_c + 2 * heads :],
    )


def solution(mesh):
    rows = P(("dp", "tensor"), None)
    specs = (
        P("dp", "tensor"), P("dp", "tensor"), P("dp", None), P("dp", "tensor"),
        P("tensor", "dp"), P("dp"), P(None, "tensor", "dp"), P("tensor", "dp"),
        P(None, "dp"), P("dp"), P("tensor", "dp"), P("tensor"), P("tensor"), P("tensor"),
    )
    return jax.shard_map(
        shards,
        mesh=mesh,
        in_specs=(rows, P("dp"), rows) + specs,
        out_specs=(rows, rows) + specs,
        check_vma=False,
    )
```
